512 devices in a mesh: segment: 4 (over z_lo), dp: 128 (over z_hi, y, x, core).
Axes of the slice: x: 4, y: 8, z: 8 (z_hi: 2, z_lo: 4; z = z_hi * 4 + z_lo), core: 2. Of those that a mesh axis runs over, the one named last changes fastest.
Arguments:
- hidden: bfloat16 [4, 256, 7168], P('segment', 'dp')
- head_weight: bfloat16 [65536, 7168], P(('segment', 'dp')), as said below
- target_ids: int32 [4, 256], P('segment', 'dp'), may hold values from 0 to 65535
- policy_logp: float32 [4, 256], P('segment', 'dp'), may hold values from -20 to -10
Outputs:
- ref_logp: float32 [4, 256], P('segment', 'dp')
- kl_term: float32 [4, 256], P('segment', 'dp')
The draws below stay inside these ranges and needn't reach their ends.
Inputs may be any that keep to these rules, and one draw needn't show every extreme that they name: `head_weight`: each vocabulary row of the head is drawn on its own.
All inputs are finite; a program needn't handle non-finite values.
Results may differ from the reference program's by a relative error of at most 0.0006.
Values may be sent and summed in bfloat16 or wider, within the bound.
No kernel may reach another device: no remote copies, remote signals or barrier semaphores. Data moves between devices by JAX's collectives and lax.ppermute only.
A program may use at most 128 MiB of HBM per device.

```python
import math
import jax
import jax.numpy as jnp
from jax import lax

D = 7168
VOCAB = 65536
MB = 4
ROWS = 256


def head_rows(key, indices):

    def one_row(index):
        row_key = jax.random.fold_in(key, index)
        values = jnp.clip(jax.random.normal(jax.random.fold_in(row_key, 1), (D,), jnp.float32), -6.0, 6.0)
        return values * (3.0 / math.sqrt(D))
    return jax.vmap(one_row)(indices)


def draw_head_weight(key, part):
    return head_rows(key, jnp.arange(VOCAB, dtype=jnp.int32)).astype(jnp.bfloat16)


def draw_hidden(key, part):
    own_key = jax.random.fold_in(key, 11)
    base = jnp.clip(jax.random.normal(jax.random.fold_in(own_key, 1), (MB, ROWS, D), jnp.float32), -6.0, 6.0)
    return base.astype(jnp.bfloat16)


def touch_ends(values, stream_key, smallest, top_value):
    longest = values.shape.index(max(values.shape))
    spots = []
    for shift in (0, 1):
        where = [jax.random.randint(jax.random.fold_in(stream_key, axis), (), 0, length) for axis, length in enumerate(values.shape)]
        where[longest] = (where[longest] + shift) % values.shape[longest]
        spots.append(tuple(where))
    return values.at[spots[0]].set(smallest).at[spots[1]].set(top_value)


def shard_levels(rng, dims, cuts, smallest, high):
    level = 1.0
    for dim, shards_of in cuts:
        heights = jax.random.uniform(jax.random.fold_in(jax.random.fold_in(rng, 6), dim), (shards_of,), jnp.float32, smallest / len(cuts), high / len(cuts))
        level = level * jnp.repeat(jnp.exp(heights), dims[dim] // shards_of).reshape((-1,) + (1,) * (len(dims) - 1 - dim))
    return level


def setup_inputs(seed: int = 0) -> dict:
    key_of = jax.random.split(jax.random.key(seed), 5)
    return {
        "hidden": draw_hidden(jax.random.fold_in(key_of[4], 71), 0),
        "head_weight": draw_head_weight(jax.random.fold_in(key_of[4], 71), 0),
        "target_ids": touch_ends(jax.random.randint(key_of[2], (MB, ROWS), 0, VOCAB), jax.random.fold_in(key_of[2], 1), 0, VOCAB - 1).astype(jnp.int32),
        "policy_logp": jnp.clip(-20.0 + 10.0 * jax.random.uniform(key_of[3], (MB, ROWS), jnp.float32) ** shard_levels(key_of[3], (MB, ROWS), ((0, 4), (1, 128)), -0.2, 0.2), -20.0, -10.0),
    }


def reference(hidden, head_weight, target_ids, policy_logp):
    def score_batch(operands):
        batch_rows, batch_ids = operands
        logits = jnp.dot(batch_rows, head_weight.T, preferred_element_type=jnp.float32)
        highest = jnp.max(logits, axis=1)
        totals = jnp.sum(jnp.exp(logits - highest[:, None]), axis=1)
        picked = jnp.take_along_axis(logits, batch_ids[:, None].astype(jnp.int32), axis=1)[:, 0]
        return picked - (highest + jnp.log(totals))

    ref_logp = lax.map(score_batch, (hidden, target_ids))
    log_ratio = ref_logp - policy_logp
    kl_term = jnp.minimum(jnp.exp(log_ratio) - log_ratio - 1.0, 10.0)
    return ref_logp, kl_term
```

```python
import functools
import jax
import jax.numpy as jnp
import numpy as np
from jax import lax
from jax.experimental import pallas as pl
from jax.experimental.pallas import tpu as pltpu
from jax.sharding import Mesh, PartitionSpec as P

NAMES = ("s1", "s0", "zh", "y1", "y0", "x", "core")
SIZES = (2, 2, 2, 4, 2, 4, 2)
SEG = ("s1", "s0")
DP = ("zh", "y1", "y0", "x", "core")
KG = ("s0", "y0")
GA = ("s1", "zh", "y1")
GB = ("x",)
IDS = 128


def size_of(axes):
    return int(np.prod([SIZES[NAMES.index(a)] for a in axes]))


def matmul_kernel(h_ref, own_ref, other_ref, out_ref):
    depth = own_ref.shape[1]
    half = own_ref.shape[0]
    rows = h_ref[:, 0, :, :depth].reshape(-1, depth)
    dims = (((1,), (1,)), ((), ()))
    out_ref[0, :, :half] = lax.dot_general(
        rows, own_ref[...], dims, preferred_element_type=jnp.float32
    )
    out_ref[0, :, half:] = lax.dot_general(
        rows, other_ref[...], dims, preferred_element_type=jnp.float32
    )


def partial_logits(gathered, own, other):
    nb, nk, rows, width = gathered.shape
    voc, depth = own.shape
    return pl.pallas_call(
        matmul_kernel,
        grid=(nk,),
        in_specs=[
            pl.BlockSpec((nb, 1, rows, width), lambda k: (0, k, 0, 0)),
            pl.BlockSpec((voc, depth), lambda k: (0, 0)),
            pl.BlockSpec((voc, depth), lambda k: (0, 0)),
        ],
        out_specs=pl.BlockSpec((1, nb * rows, 2 * voc), lambda k: (k, 0, 0)),
        out_shape=jax.ShapeDtypeStruct((nk, nb * rows, 2 * voc), jnp.float32),
        compiler_params=pltpu.CompilerParams(vmem_limit_bytes=48 * 1024 * 1024),
    )(gathered, own, other)


def stats_kernel(parts_ref, ids_ref, columns_ref, out_ref):
    nk = parts_ref.shape[0]
    logits = parts_ref[0]
    for k in range(1, nk):
        logits = logits + parts_ref[k]
    top = jnp.max(logits, axis=1, keepdims=True)
    total = jnp.sum(jnp.exp(logits - top), axis=1, keepdims=True)
    hit = ids_ref[...] == columns_ref[...]
    picked = jnp.sum(jnp.where(hit, logits, 0.0), axis=1, keepdims=True)
    lane = lax.broadcasted_iota(jnp.int32, out_ref.shape, 1)
    out_ref[...] = jnp.where(lane == 0, top, jnp.where(lane == 1, total, picked))


def local_stats(parts, ids, columns):
    return pl.pallas_call(
        stats_kernel,
        out_shape=jax.ShapeDtypeStruct((parts.shape[1], 128), jnp.float32),
        compiler_params=pltpu.CompilerParams(vmem_limit_bytes=32 * 1024 * 1024),
    )(parts, ids, columns)


def per_device(hidden, head_weight, target_ids, policy_logp):
    nk, na, nb = size_of(KG), size_of(GA), size_of(GB)
    rows, width = hidden.shape[1:]
    voc = head_weight.shape[0]
    depth = width // nk
    k_index = lax.axis_index(KG)
    core = lax.axis_index("core")

    slices = hidden.reshape(rows, nk, depth).transpose(1, 0, 2)
    ids = target_ids.reshape(rows, 1)
    lane = lax.broadcasted_iota(jnp.int32, (rows, IDS), 1)
    code = jnp.where(lane == 0, ids // 256, ids % 256).astype(hidden.dtype)
    code = jnp.broadcast_to(code[None], (nk, rows, IDS))
    message = jnp.concatenate([slices, code], axis=2)
    message = jnp.broadcast_to(message[:, None], (nk, na, rows, depth + IDS))
    message = message.reshape(nk * na, rows, depth + IDS)
    column = lax.all_to_all(message, KG + GA, 0, 0, tiled=True)
    column = column.reshape(nk * na * rows, depth + IDS)
    gathered = lax.all_gather(column, GB, axis=0, tiled=True)
    gathered = gathered.reshape(nb, nk, na * rows, depth + IDS)

    pieces = head_weight.reshape(voc, nk, depth).transpose(1, 0, 2)
    own = lax.all_to_all(pieces, KG, 0, 0, tiled=True).reshape(nk * voc, depth)
    other = lax.ppermute(own, "core", [(0, 1), (1, 0)])

    parts = partial_logits(gathered, own, other)
    parts = lax.all_to_all(parts, KG, 0, 0, tiled=True)

    def device(c, k0, k1):
        at = {a: lax.axis_index(a) for a in NAMES}
        at.update({"core": c, KG[0]: k0, KG[1]: k1})
        flat = 0
        for a, n in zip(NAMES, SIZES):
            flat = flat * n + at[a]
        return flat

    cell = jnp.arange(2 * nk, dtype=jnp.int32)
    n1 = size_of(KG[1:])
    first = device(
        jnp.where(cell < nk, core, 1 - core), (cell % nk) // n1, cell % n1
    )
    columns = (first[:, None] * voc + jnp.arange(voc, dtype=jnp.int32)).reshape(1, -1)
    mine = lax.dynamic_slice_in_dim(gathered, k_index, 1, 1)[:, 0, :, depth : depth + 2]
    mine = mine.astype(jnp.int32).reshape(nb * na * rows, 2)
    mine = mine[:, :1] * 256 + mine[:, 1:]

    stats = local_stats(parts, mine, columns)[:, :8]
    stats = stats.reshape(nb * na, rows, 8)
    stats = lax.all_to_all(stats, GB + GA, 0, 0, tiled=True)
    tops, totals, picks = stats[..., 0], stats[..., 1], stats[..., 2]
    highest = jnp.max(tops, axis=0)
    total = jnp.sum(totals * jnp.exp(tops - highest), axis=0)
    picked = jnp.sum(picks, axis=0)
    ref_logp = (picked - (highest + jnp.log(total))).reshape(1, rows)
    log_ratio = ref_logp - policy_logp
    kl_term = jnp.minimum(jnp.exp(log_ratio) - log_ratio - 1.0, 10.0)
    return (ref_logp, kl_term)


def solution(mesh):
    fine = Mesh(mesh.devices.reshape(SIZES), NAMES)
    return jax.shard_map(
        per_device,
        mesh=fine,
        in_specs=(P(SEG, DP, None), P(SEG + DP, None), P(SEG, DP), P(SEG, DP)),
        out_specs=(P(SEG, DP), P(SEG, DP)),
        check_vma=False,
    )
```

```python
import jax
import jax.numpy as jnp
import numpy as np
from jax import lax
from jax.experimental import pallas as pl
from jax.experimental.pallas import tpu as pltpu
from jax.sharding import Mesh, PartitionSpec as P

NAMES = ("s1", "s0", "zh", "y1", "y0", "x", "core")
SIZES = (2, 2, 2, 4, 2, 4, 2)
SEG = ("s1", "s0")
DP = ("zh", "y1", "y0", "x", "core")
GA = ("s1", "zh", "y1")
GB = ("x",)
IDS = 128
SWAP = [(0, 1), (1, 0)]


def size_of(axes):
    return int(np.prod([SIZES[NAMES.index(a)] for a in axes]))


def matmul_kernel(s0_ref, h_ref, *refs):
    pieces, (keep_ref, send_ref, id_ref) = refs[:-3], refs[-3:]
    voc, depth = pieces[0].shape
    mine = s0_ref[0]
    wide = h_ref.shape[-1]
    kept = h_ref[:, mine].reshape(-1, wide)
    sent = h_ref[:, 1 - mine].reshape(-1, wide)
    rows = jnp.concatenate([kept[:, :depth], sent[:, :depth]], axis=0)
    half = kept.shape[0]
    code = kept[:, depth:].astype(jnp.float32).T
    id_ref[...] = (code[0:1] * 256.0 + code[1:2]).astype(jnp.int32)
    for j, piece in enumerate(pieces):
        out = lax.dot_general(
            piece[...], rows, (((1,), (1,)), ((), ())),
            preferred_element_type=jnp.float32,
        )
        keep_ref[j] = out[:, :half]
        send_ref[j ^ 1] = out[:, half:]


def partial_logits(s0, gathered, pieces):
    nb, _, rows, _ = gathered.shape
    voc = pieces[0].shape[0]
    block = jax.ShapeDtypeStruct((len(pieces), voc, nb * rows), jnp.float32)
    vmem = pl.BlockSpec(memory_space=pltpu.VMEM)
    return pl.pallas_call(
        matmul_kernel,
        in_specs=[pl.BlockSpec(memory_space=pltpu.SMEM)] + [vmem] * (1 + len(pieces)),
        out_specs=[vmem] * 3,
        out_shape=[block, block, jax.ShapeDtypeStruct((1, nb * rows), jnp.int32)],
        compiler_params=pltpu.CompilerParams(vmem_limit_bytes=48 * 1024 * 1024),
    )(s0, gathered, *pieces)


def stats_kernel(first_ref, mine_ref, theirs_ref, ids_ref, out_ref):
    pieces, voc, rows = mine_ref.shape
    logits = mine_ref[...] + theirs_ref[...]
    top = jnp.max(jnp.max(logits, axis=0), axis=0, keepdims=True)
    total = jnp.sum(jnp.sum(jnp.exp(logits - top[None]), axis=0), axis=0, keepdims=True)
    ids = ids_ref[...]
    entry = lax.broadcasted_iota(jnp.int32, (voc, rows), 0)
    picked = jnp.zeros((voc, rows), jnp.float32)
    for j in range(pieces):
        picked += jnp.where(entry + first_ref[j] == ids, logits[j], 0.0)
    picked = jnp.sum(picked, axis=0, keepdims=True)
    line = lax.broadcasted_iota(jnp.int32, (128, rows), 0)
    out_ref[...] = jnp.where(line == 0, top, jnp.where(line == 1, total, picked)).T


def local_stats(first, mine, theirs, ids):
    vmem = pl.BlockSpec(memory_space=pltpu.VMEM)
    return pl.pallas_call(
        stats_kernel,
        in_specs=[pl.BlockSpec(memory_space=pltpu.SMEM)] + [vmem] * 3,
        out_specs=vmem,
        out_shape=jax.ShapeDtypeStruct((mine.shape[2], 128), jnp.float32),
        compiler_params=pltpu.CompilerParams(vmem_limit_bytes=32 * 1024 * 1024),
    )(first, mine, theirs, ids)


def per_device(hidden, head_weight, target_ids, policy_logp):
    na, nb = size_of(GA), size_of(GB)
    rows, width = hidden.shape[1:]
    voc = head_weight.shape[0]
    depth = width // 2
    at = {a: lax.axis_index(a) for a in NAMES}
    s0 = at["s0"]

    kept = lax.dynamic_slice_in_dim(head_weight, s0 * depth, depth, 1)
    given = lax.dynamic_slice_in_dim(head_weight, (1 - s0) * depth, depth, 1)
    pieces = [
        kept,
        lax.ppermute(given, "s0", SWAP),
        lax.ppermute(kept, "y0", SWAP),
        lax.ppermute(given, ("s0", "y0"), [(i, i ^ 3) for i in range(4)]),
    ]

    ids = target_ids.reshape(rows, 1)
    lane = lax.broadcasted_iota(jnp.int32, (rows, IDS), 1)
    code = jnp.where(lane == 0, ids >> 8, ids & 255).astype(hidden.dtype)
    halves = [
        jnp.concatenate([hidden[0, :, k * depth : (k + 1) * depth], code], axis=1)
        for k in range(2)
    ]
    message = jnp.broadcast_to(jnp.stack(halves)[:, None], (2, na, rows, depth + IDS))
    message = message.reshape(2 * na, rows, depth + IDS)
    column = lax.all_to_all(message, ("s0",) + GA, 0, 0, tiled=True)
    column = column.reshape(2 * na * rows, depth + IDS)
    copies = jnp.broadcast_to(column[None], (nb,) + column.shape)
    gathered = lax.all_to_all(copies, GB, 0, 0, tiled=True)
    gathered = gathered.reshape(nb, 2, na * rows, depth + IDS)

    pieces += [lax.ppermute(piece, "core", SWAP) for piece in pieces]

    mine, send, ids = partial_logits(s0.reshape(1), gathered, pieces)
    theirs = lax.ppermute(send, "s0", SWAP)

    firsts = []
    for j in range(len(pieces)):
        place = dict(at)
        place["s0"] = at["s0"] ^ (j & 1)
        place["y0"] = at["y0"] ^ ((j >> 1) & 1)
        place["core"] = at["core"] ^ (j >> 2)
        flat = 0
        for a, n in zip(NAMES, SIZES):
            flat = flat * n + place[a]
        firsts.append(flat * voc)
    stats = local_stats(jnp.stack(firsts), mine, theirs, ids)[:, :8]
    stats = stats.reshape(nb * na, rows, 8)
    stats = lax.all_to_all(stats, GB + GA, 0, 0, tiled=True)
    tops, totals, picks = stats[..., 0], stats[..., 1], stats[..., 2]
    highest = jnp.max(tops, axis=0)
    total = jnp.sum(totals * jnp.exp(tops - highest), axis=0)
    picked = jnp.sum(picks, axis=0)
    ref_logp = (picked - (highest + jnp.log(total))).reshape(1, rows)
    log_ratio = ref_logp - policy_logp
    kl_term = jnp.minimum(jnp.exp(log_ratio) - log_ratio - 1.0, 10.0)
    return (ref_logp, kl_term)


def solution(mesh):
    fine = Mesh(mesh.devices.reshape(SIZES), NAMES)
    return jax.shard_map(
        per_device,
        mesh=fine,
        in_specs=(P(SEG, DP, None), P(SEG + DP, None), P(SEG, DP), P(SEG, DP)),
        out_specs=(P(SEG, DP), P(SEG, DP)),
        check_vma=False,
    )
```

```python
import jax
import jax.numpy as jnp
import numpy as np
from jax import lax
from jax.experimental import pallas as pl
from jax.experimental.pallas import tpu as pltpu
from jax.sharding import Mesh, PartitionSpec as P

NAMES = ("s1", "s0", "zh", "y1", "y0", "x1", "x0", "core")
SIZES = (2, 2, 2, 4, 2, 2, 2, 2)
SEG = ("s1", "s0")
DP = ("zh", "y1", "y0", "x1", "x0", "core")
GA = ("s1", "zh", "y1")
GB = ("s0", "y0")
IDS = 128
SWAP = [(0, 1), (1, 0)]


def size_of(axes):
    return int(np.prod([SIZES[NAMES.index(a)] for a in axes]))


def halves_kernel(k_ref, weight_ref, kept_ref, given_ref, sems):
    depth = kept_ref.shape[1]
    mine = pl.multiple_of(k_ref[0] * depth, 128)
    rest = pl.multiple_of((1 - k_ref[0]) * depth, 128)
    copies = [
        pltpu.make_async_copy(weight_ref.at[:, pl.ds(mine, depth)], kept_ref, sems.at[0]),
        pltpu.make_async_copy(weight_ref.at[:, pl.ds(rest, depth)], given_ref, sems.at[1]),
    ]
    for copy in copies:
        copy.start()
    for copy in copies:
        copy.wait()


def halves_of(k, weight):
    half = jax.ShapeDtypeStruct((weight.shape[0], weight.shape[1] // 2), weight.dtype)
    anywhere = pl.BlockSpec(memory_space=pl.ANY)
    return pl.pallas_call(
        halves_kernel,
        in_specs=[pl.BlockSpec(memory_space=pltpu.SMEM), anywhere],
        out_specs=[anywhere] * 2,
        out_shape=[half, half],
        scratch_shapes=[pltpu.SemaphoreType.DMA((2,))],
        compiler_params=pltpu.CompilerParams(vmem_limit_bytes=56 * 1024 * 1024),
    )(k, weight)


def matmul_kernel(*refs):
    h_ref, pieces, (keep_ref, send_ref, id_ref) = refs[0], refs[1:9], refs[9:12]
    rows_in, held, turned, keep, send, row_sems, sems, keep_sems, send_sems = refs[12:]
    depth = pieces[0].shape[1]
    wide = h_ref.shape[-1]
    arrivals = [
        pltpu.make_async_copy(h_ref.at[b], rows_in.at[b], row_sems.at[b])
        for b in range(h_ref.shape[0])
    ]
    loads = [
        pltpu.make_async_copy(piece, held.at[j], sems.at[j])
        for j, piece in enumerate(pieces)
    ]
    for copy in arrivals + loads:
        copy.start()
    for copy in arrivals:
        copy.wait()
    kept = rows_in[:, 0].reshape(-1, wide)
    sent = rows_in[:, 1].reshape(-1, wide)
    half = kept.shape[0]
    turned[:, :half] = kept[:, :depth].T
    turned[:, half:] = sent[:, :depth].T
    code = kept[:, depth:].astype(jnp.float32).T
    id_ref[...] = (code[0:1] * 256.0 + code[1:2]).astype(jnp.int32)
    stores = []
    for j, load in enumerate(loads):
        load.wait()
        out = jnp.dot(held[j], turned[...], preferred_element_type=jnp.float32)
        send[j ^ 1] = out[:, half:]
        keep[j] = out[:, :half]
        stores += [
            pltpu.make_async_copy(send.at[j ^ 1], send_ref.at[j ^ 1], send_sems.at[j]),
            pltpu.make_async_copy(keep.at[j], keep_ref.at[j], keep_sems.at[j]),
        ]
        stores[-2].start()
        stores[-1].start()
    for copy in stores:
        copy.wait()


def partial_logits(gathered, pieces):
    nb, _, rows, _ = gathered.shape
    voc, depth = pieces[0].shape
    block = jax.ShapeDtypeStruct((len(pieces), voc, nb * rows), jnp.float32)
    anywhere = pl.BlockSpec(memory_space=pl.ANY)
    count = len(pieces)
    return pl.pallas_call(
        matmul_kernel,
        in_specs=[anywhere] * (1 + count),
        out_specs=[anywhere, anywhere, pl.BlockSpec(memory_space=pltpu.VMEM)],
        out_shape=[block, block, jax.ShapeDtypeStruct((1, nb * rows), jnp.int32)],
        scratch_shapes=[
            pltpu.VMEM(gathered.shape, gathered.dtype),
            pltpu.VMEM((count, voc, depth), gathered.dtype),
            pltpu.VMEM((depth, 2 * nb * rows), gathered.dtype),
            pltpu.VMEM(block.shape, jnp.float32),
            pltpu.VMEM(block.shape, jnp.float32),
            pltpu.SemaphoreType.DMA((nb,)),
            pltpu.SemaphoreType.DMA((count,)),
            pltpu.SemaphoreType.DMA((count,)),
            pltpu.SemaphoreType.DMA((count,)),
        ],
        compiler_params=pltpu.CompilerParams(vmem_limit_bytes=50 * 1024 * 1024),
    )(gathered, *pieces)


def stats_kernel(first_ref, mine_ref, theirs_ref, ids_ref, out_ref):
    pieces, voc, rows = mine_ref.shape
    logits = mine_ref[...] + theirs_ref[...]
    top = jnp.max(jnp.max(logits, axis=0), axis=0, keepdims=True)
    total = jnp.sum(jnp.sum(jnp.exp(logits - top[None]), axis=0), axis=0, keepdims=True)
    ids = ids_ref[...]
    entry = lax.broadcasted_iota(jnp.int32, (voc, rows), 0)
    picked = jnp.zeros((voc, rows), jnp.float32)
    for j in range(pieces):
        picked += jnp.where(entry + first_ref[j] == ids, logits[j], 0.0)
    picked = jnp.sum(picked, axis=0, keepdims=True)
    line = lax.broadcasted_iota(jnp.int32, (128, rows), 0)
    out_ref[...] = jnp.where(line == 0, top, jnp.where(line == 1, total, picked)).T


def local_stats(first, mine, theirs, ids):
    vmem = pl.BlockSpec(memory_space=pltpu.VMEM)
    return pl.pallas_call(
        stats_kernel,
        in_specs=[pl.BlockSpec(memory_space=pltpu.SMEM)] + [vmem] * 3,
        out_specs=vmem,
        out_shape=jax.ShapeDtypeStruct((mine.shape[2], 128), jnp.float32),
        compiler_params=pltpu.CompilerParams(vmem_limit_bytes=8 * 1024 * 1024),
    )(first, mine, theirs, ids)


def per_device(hidden, head_weight, target_ids, policy_logp):
    na, nb = size_of(GA), size_of(GB)
    rows, width = hidden.shape[1:]
    voc = head_weight.shape[0]
    depth = width // 2
    at = {a: lax.axis_index(a) for a in NAMES}
    k = at["x0"]

    ids = target_ids.reshape(rows, 1)
    lane = lax.broadcasted_iota(jnp.int32, (rows, IDS), 1)
    code = jnp.where(lane == 0, ids >> 8, ids & 255).astype(hidden.dtype)
    low, high = hidden[0, :, :depth], hidden[0, :, depth:]
    own = jnp.concatenate([jnp.where(k == 0, low, high), code], axis=1)
    other = jnp.concatenate([jnp.where(k == 0, high, low), code], axis=1)
    other = lax.ppermute(other, "x0", SWAP)

    kept, given = halves_of(k.reshape(1), head_weight)
    near = lax.ppermute(given, "x0", SWAP)
    back = lax.ppermute(given, ("x1", "x0"), [(i, i ^ 3) for i in range(4)])

    message = jnp.broadcast_to(jnp.stack([own, other])[None], (na, 2, rows, depth + IDS))
    column = lax.all_to_all(message, GA, 0, 0, tiled=True)
    column = column.transpose(1, 0, 2, 3).reshape(2 * na * rows, depth + IDS)
    column, near, back = lax.optimization_barrier((column, near, back))
    copies = jnp.broadcast_to(column[None], (nb,) + column.shape)
    gathered = lax.all_to_all(copies, GB, 0, 0, tiled=True)
    gathered = gathered.reshape(nb, 2, na * rows, depth + IDS)

    pieces = [kept, near, lax.ppermute(kept, "x1", SWAP), back]
    pieces += [lax.ppermute(piece, "core", SWAP) for piece in pieces]

    mine, send, ids = partial_logits(gathered, pieces)
    theirs = lax.ppermute(send, "x0", SWAP)

    firsts = []
    for j in range(len(pieces)):
        place = dict(at)
        place["x0"] = at["x0"] ^ (j & 1)
        place["x1"] = at["x1"] ^ ((j >> 1) & 1)
        place["core"] = at["core"] ^ (j >> 2)
        flat = 0
        for a, n in zip(NAMES, SIZES):
            flat = flat * n + place[a]
        firsts.append(flat * voc)
    stats = local_stats(jnp.stack(firsts), mine, theirs, ids)[:, :8]
    stats = stats.reshape(nb * na, rows, 8)
    stats = lax.all_to_all(stats, GB + GA, 0, 0, tiled=True)
    tops, totals, picks = stats[..., 0], stats[..., 1], stats[..., 2]
    highest = jnp.max(tops, axis=0)
    total = jnp.sum(totals * jnp.exp(tops - highest), axis=0)
    picked = jnp.sum(picks, axis=0)
    ref_logp = (picked - (highest + jnp.log(total))).reshape(1, rows)
    log_ratio = ref_logp - policy_logp
    kl_term = jnp.minimum(jnp.exp(log_ratio) - log_ratio - 1.0, 10.0)
    return (ref_logp, kl_term)


def solution(mesh):
    fine = Mesh(mesh.devices.reshape(SIZES), NAMES)
    return jax.shard_map(
        per_device,
        mesh=fine,
        in_specs=(P(SEG, DP, None), P(SEG + DP, None), P(SEG, DP), P(SEG, DP)),
        out_specs=(P(SEG, DP), P(SEG, DP)),
        check_vma=False,
    )
```

```python
import jax
import jax.numpy as jnp
import numpy as np
from jax import lax
from jax.experimental import pallas as pl
from jax.experimental.pallas import tpu as pltpu
from jax.sharding import Mesh, PartitionSpec as P

NAMES = ("s1", "s0", "zh", "y1", "y0", "x1", "x0", "core")
SIZES = (2, 2, 2, 4, 2, 2, 2, 2)
SEG = ("s1", "s0")
DP = ("zh", "y1", "y0", "x1", "x0", "core")
GA = ("s1", "zh", "y1")
GB = ("s0", "y0")
KG = ("x1", "x0")
IDS = 128
SWAP = [(0, 1), (1, 0)]


def size_of(axes):
    return int(np.prod([SIZES[NAMES.index(a)] for a in axes]))


def matmul_kernel(x_ref, *refs):
    h_ref, pieces, (out_ref, id_ref) = refs[0], refs[1:9], refs[9:11]
    rows_in, held, turned, parts, row_sems, sems, out_sems = refs[11:]
    x = x_ref[0]
    depth = pieces[0].shape[1]
    nb, nk, _, wide = rows_in.shape
    arrivals = [
        pltpu.make_async_copy(h_ref.at[b], rows_in.at[b], row_sems.at[b])
        for b in range(nb)
    ]
    loads = [
        pltpu.make_async_copy(piece, held.at[j], sems.at[j])
        for j, piece in enumerate(pieces)
    ]
    for copy in arrivals + loads:
        copy.start()
    for copy in arrivals:
        copy.wait()
    for k in range(nk):
        rows = rows_in[:, k, :, :depth].reshape(-1, depth)
        width = rows.shape[0]
        turned[:, k * width : (k + 1) * width] = rows.T
    code = rows_in[:, x, :, depth:].reshape(-1, wide - depth).astype(jnp.float32).T
    id_ref[...] = (code[0:1] * 256.0 + code[1:2]).astype(jnp.int32)
    stores = []
    for j, load in enumerate(loads):
        load.wait()
        out = jnp.dot(held[j], turned[...], preferred_element_type=jnp.float32)
        slot = nk * (j // nk) + (x ^ (j % nk))
        for k in range(nk):
            parts[k, slot] = out[:, k * width : (k + 1) * width]
        stores.append(
            pltpu.make_async_copy(parts.at[:, slot], out_ref.at[:, slot], out_sems.at[j])
        )
        stores[-1].start()
    for copy in stores:
        copy.wait()


def partial_logits(x, gathered, pieces):
    nb, nk, rows, _ = gathered.shape
    voc, depth = pieces[0].shape
    count = len(pieces)
    block = (nk, count, voc, nb * rows)
    anywhere = pl.BlockSpec(memory_space=pl.ANY)
    return pl.pallas_call(
        matmul_kernel,
        in_specs=[pl.BlockSpec(memory_space=pltpu.SMEM)] + [anywhere] * (1 + count),
        out_specs=[anywhere, pl.BlockSpec(memory_space=pltpu.VMEM)],
        out_shape=[
            jax.ShapeDtypeStruct(block, jnp.float32),
            jax.ShapeDtypeStruct((1, nb * rows), jnp.int32),
        ],
        scratch_shapes=[
            pltpu.VMEM(gathered.shape, gathered.dtype),
            pltpu.VMEM((count, voc, depth), gathered.dtype),
            pltpu.VMEM((depth, nk * nb * rows), gathered.dtype),
            pltpu.VMEM(block, jnp.float32),
            pltpu.SemaphoreType.DMA((nb,)),
            pltpu.SemaphoreType.DMA((count,)),
            pltpu.SemaphoreType.DMA((count,)),
        ],
        compiler_params=pltpu.CompilerParams(vmem_limit_bytes=50 * 1024 * 1024),
    )(x, gathered, *pieces)


def stats_kernel(first_ref, parts_ref, ids_ref, out_ref):
    nk, pieces, voc, rows = parts_ref.shape
    logits = parts_ref[0]
    for k in range(1, nk):
        logits += parts_ref[k]
    top = jnp.max(jnp.max(logits, axis=0), axis=0, keepdims=True)
    total = jnp.sum(jnp.sum(jnp.exp(logits - top[None]), axis=0), axis=0, keepdims=True)
    ids = ids_ref[...]
    entry = lax.broadcasted_iota(jnp.int32, (voc, rows), 0)
    picked = jnp.zeros((voc, rows), jnp.float32)
    for j in range(pieces):
        picked += jnp.where(entry + first_ref[j] == ids, logits[j], 0.0)
    picked = jnp.sum(picked, axis=0, keepdims=True)
    line = lax.broadcasted_iota(jnp.int32, (128, rows), 0)
    out_ref[...] = jnp.where(line == 0, top, jnp.where(line == 1, total, picked)).T


def local_stats(first, parts, ids):
    vmem = pl.BlockSpec(memory_space=pltpu.VMEM)
    return pl.pallas_call(
        stats_kernel,
        in_specs=[pl.BlockSpec(memory_space=pltpu.SMEM), vmem, vmem],
        out_specs=vmem,
        out_shape=jax.ShapeDtypeStruct((parts.shape[3], 128), jnp.float32),
        compiler_params=pltpu.CompilerParams(vmem_limit_bytes=8 * 1024 * 1024),
    )(first, parts, ids)


def per_device(hidden, head_weight, target_ids, policy_logp):
    na, nb, nk = size_of(GA), size_of(GB), size_of(KG)
    rows, width = hidden.shape[1:]
    voc = head_weight.shape[0]
    depth = width // nk
    at = {a: lax.axis_index(a) for a in NAMES}
    x = lax.axis_index(KG)

    ids = target_ids.reshape(rows, 1)
    lane = lax.broadcasted_iota(jnp.int32, (rows, IDS), 1)
    code = jnp.where(lane == 0, ids >> 8, ids & 255).astype(hidden.dtype)
    quarters = [
        jnp.concatenate([hidden[0, :, j * depth : (j + 1) * depth], code], axis=1)
        for j in range(nk)
    ]
    quarter = lax.all_to_all(jnp.stack(quarters), KG, 0, 0, tiled=True)
    quarter = quarter.reshape(nk * rows, depth + IDS)

    def far(j):
        piece = lax.dynamic_slice_in_dim(head_weight, (x ^ j) * depth, depth, 1)
        if j == 0:
            return piece
        return lax.ppermute(piece, KG, [(i, i ^ j) for i in range(nk)])

    pieces = [far(j) for j in range(nk)]

    message = jnp.broadcast_to(quarter[None], (na,) + quarter.shape)
    column = lax.all_to_all(message, GA, 0, 0, tiled=True)
    column = column.reshape(na, nk, rows, depth + IDS).transpose(1, 0, 2, 3)
    column = column.reshape(nk * na * rows, depth + IDS)
    column, pieces[1], pieces[3] = lax.optimization_barrier((column, pieces[1], pieces[3]))
    copies = jnp.broadcast_to(column[None], (nb,) + column.shape)
    gathered = lax.all_to_all(copies, GB, 0, 0, tiled=True)
    gathered = gathered.reshape(nb, nk, na * rows, depth + IDS)

    pieces += [lax.ppermute(piece, "core", SWAP) for piece in pieces]

    parts, ids = partial_logits(x.reshape(1), gathered, pieces)
    parts = lax.all_to_all(parts, KG, 0, 0, tiled=True)

    firsts = []
    for j in range(len(pieces)):
        place = dict(at)
        place["x1"], place["x0"] = (j >> 1) & 1, j & 1
        place["core"] = at["core"] ^ (j // nk)
        flat = 0
        for a, n in zip(NAMES, SIZES):
            flat = flat * n + place[a]
        firsts.append(flat * voc)
    stats = local_stats(jnp.stack(firsts), parts, ids)[:, :8]
    stats = stats.reshape(nb * na, rows, 8)
    stats = lax.all_to_all(stats, GB + GA, 0, 0, tiled=True)
    tops, totals, picks = stats[..., 0], stats[..., 1], stats[..., 2]
    highest = jnp.max(tops, axis=0)
    total = jnp.sum(totals * jnp.exp(tops - highest), axis=0)
    picked = jnp.sum(picks, axis=0)
    ref_logp = (picked - (highest + jnp.log(total))).reshape(1, rows)
    log_ratio = ref_logp - policy_logp
    kl_term = jnp.minimum(jnp.exp(log_ratio) - log_ratio - 1.0, 10.0)
    return (ref_logp, kl_term)


def solution(mesh):
    fine = Mesh(mesh.devices.reshape(SIZES), NAMES)
    return jax.shard_map(
        per_device,
        mesh=fine,
        in_specs=(P(SEG, DP, None), P(SEG + DP, None), P(SEG, DP), P(SEG, DP)),
        out_specs=(P(SEG, DP), P(SEG, DP)),
        check_vma=False,
    )
```

```python
import jax
import jax.numpy as jnp
import numpy as np
from jax import lax
from jax.experimental import pallas as pl
from jax.experimental.pallas import tpu as pltpu
from jax.sharding import Mesh, PartitionSpec as P

NAMES = ("s1", "s0", "zh", "y1", "y0", "x1", "x0", "core")
SIZES = (2, 2, 2, 4, 2, 2, 2, 2)
SEG = ("s1", "s0")
DP = ("zh", "y1", "y0", "x1", "x0", "core")
GA = ("s1", "zh", "y1")
GB = ("s0", "y0")
IDS = 128
SWAP = [(0, 1), (1, 0)]


def size_of(axes):
    return int(np.prod([SIZES[NAMES.index(a)] for a in axes]))


def matmul_kernel(k_ref, h_ref, *refs):
    pieces, (keep_ref, send_ref, id_ref, turned) = refs[:-4], refs[-4:]
    depth = pieces[0].shape[1]
    wide = h_ref.shape[-1]
    mine = k_ref[0]
    kept = h_ref[:, mine].reshape(-1, wide)
    sent = h_ref[:, 1 - mine].reshape(-1, wide)
    half = kept.shape[0]
    turned[:, :half] = kept[:, :depth].T
    turned[:, half:] = sent[:, :depth].T
    code = kept[:, depth:].astype(jnp.float32).T
    id_ref[...] = (code[0:1] * 256.0 + code[1:2]).astype(jnp.int32)
    for j, piece in enumerate(pieces):
        out = jnp.dot(piece[...], turned[...], preferred_element_type=jnp.float32)
        keep_ref[j] = out[:, :half]
        send_ref[j ^ 1] = out[:, half:]


def partial_logits(k, gathered, pieces):
    nb, _, rows, _ = gathered.shape
    voc, depth = pieces[0].shape
    block = jax.ShapeDtypeStruct((len(pieces), voc, nb * rows), jnp.float32)
    vmem = pl.BlockSpec(memory_space=pltpu.VMEM)
    return pl.pallas_call(
        matmul_kernel,
        in_specs=[pl.BlockSpec(memory_space=pltpu.SMEM)] + [vmem] * (1 + len(pieces)),
        out_specs=[vmem] * 3,
        out_shape=[block, block, jax.ShapeDtypeStruct((1, nb * rows), jnp.int32)],
        scratch_shapes=[pltpu.VMEM((depth, 2 * nb * rows), gathered.dtype)],
        compiler_params=pltpu.CompilerParams(vmem_limit_bytes=50 * 1024 * 1024),
    )(k, gathered, *pieces)


def stats_kernel(first_ref, mine_ref, theirs_ref, ids_ref, out_ref):
    pieces, voc, rows = mine_ref.shape
    logits = mine_ref[...] + theirs_ref[...]
    top = jnp.max(jnp.max(logits, axis=0), axis=0, keepdims=True)
    total = jnp.sum(jnp.sum(jnp.exp(logits - top[None]), axis=0), axis=0, keepdims=True)
    ids = ids_ref[...]
    entry = lax.broadcasted_iota(jnp.int32, (voc, rows), 0)
    picked = jnp.zeros((voc, rows), jnp.float32)
    for j in range(pieces):
        picked += jnp.where(entry + first_ref[j] == ids, logits[j], 0.0)
    picked = jnp.sum(picked, axis=0, keepdims=True)
    line = lax.broadcasted_iota(jnp.int32, (128, rows), 0)
    out_ref[...] = jnp.where(line == 0, top, jnp.where(line == 1, total, picked)).T


def local_stats(first, mine, theirs, ids):
    vmem = pl.BlockSpec(memory_space=pltpu.VMEM)
    return pl.pallas_call(
        stats_kernel,
        in_specs=[pl.BlockSpec(memory_space=pltpu.SMEM)] + [vmem] * 3,
        out_specs=vmem,
        out_shape=jax.ShapeDtypeStruct((mine.shape[2], 128), jnp.float32),
        compiler_params=pltpu.CompilerParams(vmem_limit_bytes=8 * 1024 * 1024),
    )(first, mine, theirs, ids)


def per_device(hidden, head_weight, target_ids, policy_logp):
    na, nb = size_of(GA), size_of(GB)
    rows, width = hidden.shape[1:]
    voc = head_weight.shape[0]
    depth = width // 2
    at = {a: lax.axis_index(a) for a in NAMES}
    k = at["x0"]

    kept = lax.dynamic_slice_in_dim(head_weight, k * depth, depth, 1)
    given = lax.dynamic_slice_in_dim(head_weight, (1 - k) * depth, depth, 1)
    pieces = [
        kept,
        lax.ppermute(given, "x0", SWAP),
        lax.ppermute(kept, "x1", SWAP),
        lax.ppermute(given, ("x1", "x0"), [(i, i ^ 3) for i in range(4)]),
    ]

    ids = target_ids.reshape(rows, 1)
    lane = lax.broadcasted_iota(jnp.int32, (rows, IDS), 1)
    code = jnp.where(lane == 0, ids >> 8, ids & 255).astype(hidden.dtype)
    halves = [
        jnp.concatenate([hidden[0, :, k * depth : (k + 1) * depth], code], axis=1)
        for k in range(2)
    ]
    message = jnp.broadcast_to(jnp.stack(halves)[:, None], (2, na, rows, depth + IDS))
    message = message.reshape(2 * na, rows, depth + IDS)
    column = lax.all_to_all(message, ("x0",) + GA, 0, 0, tiled=True)
    column = column.reshape(2 * na * rows, depth + IDS)
    copies = jnp.broadcast_to(column[None], (nb,) + column.shape)
    gathered = lax.all_to_all(copies, GB, 0, 0, tiled=True)
    gathered = gathered.reshape(nb, 2, na * rows, depth + IDS)

    pieces += [lax.ppermute(piece, "core", SWAP) for piece in pieces]

    mine, send, ids = partial_logits(k.reshape(1), gathered, pieces)
    theirs = lax.ppermute(send, "x0", SWAP)

    firsts = []
    for j in range(len(pieces)):
        place = dict(at)
        place["x0"] = at["x0"] ^ (j & 1)
        place["x1"] = at["x1"] ^ ((j >> 1) & 1)
        place["core"] = at["core"] ^ (j >> 2)
        flat = 0
        for a, n in zip(NAMES, SIZES):
            flat = flat * n + place[a]
        firsts.append(flat * voc)
    stats = local_stats(jnp.stack(firsts), mine, theirs, ids)[:, :8]
    stats = stats.reshape(nb * na, rows, 8)
    stats = lax.all_to_all(stats, GB + GA, 0, 0, tiled=True)
    tops, totals, picks = stats[..., 0], stats[..., 1], stats[..., 2]
    highest = jnp.max(tops, axis=0)
    total = jnp.sum(totals * jnp.exp(tops - highest), axis=0)
    picked = jnp.sum(picks, axis=0)
    ref_logp = (picked - (highest + jnp.log(total))).reshape(1, rows)
    log_ratio = ref_logp - policy_logp
    kl_term = jnp.minimum(jnp.exp(log_ratio) - log_ratio - 1.0, 10.0)
    return (ref_logp, kl_term)


def solution(mesh):
    fine = Mesh(mesh.devices.reshape(SIZES), NAMES)
    return jax.shard_map(
        per_device,
        mesh=fine,
        in_specs=(P(SEG, DP, None), P(SEG + DP, None), P(SEG, DP), P(SEG, DP)),
        out_specs=(P(SEG, DP), P(SEG, DP)),
        check_vma=False,
    )
```

```python
import jax
import jax.numpy as jnp
import numpy as np
from jax import lax
from jax.experimental import pallas as pl
from jax.experimental.pallas import tpu as pltpu
from jax.sharding import Mesh, PartitionSpec as P

NAMES = ("s1", "s0", "zh", "y1", "y0", "x1", "x0", "core")
SIZES = (2, 2, 2, 4, 2, 2, 2, 2)
SEG = ("s1", "s0")
DP = ("zh", "y1", "y0", "x1", "x0", "core")
GA = ("s1", "zh", "y1")
GB = ("s0", "y0")
IDS = 128
SWAP = [(0, 1), (1, 0)]


def size_of(axes):
    return int(np.prod([SIZES[NAMES.index(a)] for a in axes]))


def matmul_kernel(k_ref, h_ref, *refs):
    pieces, (keep_ref, send_ref, id_ref, turned) = refs[:-4], refs[-4:]
    depth = pieces[0].shape[1]
    wide = h_ref.shape[-1]
    mine = k_ref[0]
    kept = h_ref[:, mine].reshape(-1, wide)
    sent = h_ref[:, 1 - mine].reshape(-1, wide)
    half = kept.shape[0]
    turned[:, :half] = kept[:, :depth].T
    turned[:, half:] = sent[:, :depth].T
    code = kept[:, depth:].astype(jnp.float32).T
    id_ref[...] = (code[0:1] * 256.0 + code[1:2]).astype(jnp.int32)
    for j, piece in enumerate(pieces):
        out = jnp.dot(piece[...], turned[...], preferred_element_type=jnp.float32)
        keep_ref[j] = out[:, :half]
        send_ref[j ^ 1] = out[:, half:]


def partial_logits(k, gathered, pieces):
    nb, _, rows, _ = gathered.shape
    voc, depth = pieces[0].shape
    block = jax.ShapeDtypeStruct((len(pieces), voc, nb * rows), jnp.float32)
    vmem = pl.BlockSpec(memory_space=pltpu.VMEM)
    return pl.pallas_call(
        matmul_kernel,
        in_specs=[pl.BlockSpec(memory_space=pltpu.SMEM)] + [vmem] * (1 + len(pieces)),
        out_specs=[vmem] * 3,
        out_shape=[block, block, jax.ShapeDtypeStruct((1, nb * rows), jnp.int32)],
        scratch_shapes=[pltpu.VMEM((depth, 2 * nb * rows), gathered.dtype)],
        compiler_params=pltpu.CompilerParams(vmem_limit_bytes=50 * 1024 * 1024),
    )(k, gathered, *pieces)


def stats_kernel(first_ref, mine_ref, theirs_ref, ids_ref, out_ref):
    pieces, voc, rows = mine_ref.shape
    logits = mine_ref[...] + theirs_ref[...]
    top = jnp.max(jnp.max(logits, axis=0), axis=0, keepdims=True)
    total = jnp.sum(jnp.sum(jnp.exp(logits - top[None]), axis=0), axis=0, keepdims=True)
    ids = ids_ref[...]
    entry = lax.broadcasted_iota(jnp.int32, (voc, rows), 0)
    picked = jnp.zeros((voc, rows), jnp.float32)
    for j in range(pieces):
        picked += jnp.where(entry + first_ref[j] == ids, logits[j], 0.0)
    picked = jnp.sum(picked, axis=0, keepdims=True)
    line = lax.broadcasted_iota(jnp.int32, (128, rows), 0)
    out_ref[...] = jnp.where(line == 0, top, jnp.where(line == 1, total, picked)).T


def local_stats(first, mine, theirs, ids):
    vmem = pl.BlockSpec(memory_space=pltpu.VMEM)
    return pl.pallas_call(
        stats_kernel,
        in_specs=[pl.BlockSpec(memory_space=pltpu.SMEM)] + [vmem] * 3,
        out_specs=vmem,
        out_shape=jax.ShapeDtypeStruct((mine.shape[2], 128), jnp.float32),
        compiler_params=pltpu.CompilerParams(vmem_limit_bytes=8 * 1024 * 1024),
    )(first, mine, theirs, ids)


def per_device(hidden, head_weight, target_ids, policy_logp):
    na, nb = size_of(GA), size_of(GB)
    rows, width = hidden.shape[1:]
    voc = head_weight.shape[0]
    depth = width // 2
    at = {a: lax.axis_index(a) for a in NAMES}
    k = at["x0"]

    kept = lax.dynamic_slice_in_dim(head_weight, k * depth, depth, 1)
    given = lax.dynamic_slice_in_dim(head_weight, (1 - k) * depth, depth, 1)
    pieces = [
        kept,
        lax.ppermute(given, "x0", SWAP),
        lax.ppermute(kept, "x1", SWAP),
        lax.ppermute(given, ("x1", "x0"), [(i, i ^ 3) for i in range(4)]),
    ]

    ids = target_ids.reshape(rows, 1)
    lane = lax.broadcasted_iota(jnp.int32, (rows, IDS), 1)
    code = jnp.where(lane == 0, ids >> 8, ids & 255).astype(hidden.dtype)
    halves = [
        jnp.concatenate([hidden[0, :, k * depth : (k + 1) * depth], code], axis=1)
        for k in range(2)
    ]
    message = jnp.broadcast_to(jnp.stack(halves)[:, None], (2, na, rows, depth + IDS))
    message = message.reshape(2 * na, rows, depth + IDS)
    column = lax.all_to_all(message, ("x0",) + GA, 0, 0, tiled=True)
    column = column.reshape(2 * na * rows, depth + IDS)
    column, pieces[1], pieces[3] = lax.optimization_barrier((column, pieces[1], pieces[3]))
    copies = jnp.broadcast_to(column[None], (nb,) + column.shape)
    gathered = lax.all_to_all(copies, GB, 0, 0, tiled=True)
    gathered = gathered.reshape(nb, 2, na * rows, depth + IDS)

    near = [lax.ppermute(pieces[j], "core", SWAP) for j in (0, 1, 3)]
    pieces[2], *near = lax.optimization_barrier((pieces[2], *near))
    pieces += [near[0], near[1], lax.ppermute(pieces[2], "core", SWAP), near[2]]

    mine, send, ids = partial_logits(k.reshape(1), gathered, pieces)
    theirs = lax.ppermute(send, "x0", SWAP)

    firsts = []
    for j in range(len(pieces)):
        place = dict(at)
        place["x0"] = at["x0"] ^ (j & 1)
        place["x1"] = at["x1"] ^ ((j >> 1) & 1)
        place["core"] = at["core"] ^ (j >> 2)
        flat = 0
        for a, n in zip(NAMES, SIZES):
            flat = flat * n + place[a]
        firsts.append(flat * voc)
    stats = local_stats(jnp.stack(firsts), mine, theirs, ids)[:, :8]
    stats = stats.reshape(nb * na, rows, 8)
    stats = lax.all_to_all(stats, GB + GA, 0, 0, tiled=True)
    tops, totals, picks = stats[..., 0], stats[..., 1], stats[..., 2]
    highest = jnp.max(tops, axis=0)
    total = jnp.sum(totals * jnp.exp(tops - highest), axis=0)
    picked = jnp.sum(picks, axis=0)
    ref_logp = (picked - (highest + jnp.log(total))).reshape(1, rows)
    log_ratio = ref_logp - policy_logp
    kl_term = jnp.minimum(jnp.exp(log_ratio) - log_ratio - 1.0, 10.0)
    return (ref_logp, kl_term)


def solution(mesh):
    fine = Mesh(mesh.devices.reshape(SIZES), NAMES)
    return jax.shard_map(
        per_device,
        mesh=fine,
        in_specs=(P(SEG, DP, None), P(SEG + DP, None), P(SEG, DP), P(SEG, DP)),
        out_specs=(P(SEG, DP), P(SEG, DP)),
        check_vma=False,
    )
```

```python
import jax
import jax.numpy as jnp
import numpy as np
from jax import lax
from jax.experimental import pallas as pl
from jax.experimental.pallas import tpu as pltpu
from jax.sharding import Mesh, PartitionSpec as P

NAMES = ("s1", "s0", "zh", "y1", "y0", "x1", "x0", "core")
SIZES = (2, 2, 2, 4, 2, 2, 2, 2)
SEG = ("s1", "s0")
DP = ("zh", "y1", "y0", "x1", "x0", "core")
GA = ("s1", "zh", "y1")
GB = ("s0", "y0")
IDS = 128
SWAP = [(0, 1), (1, 0)]
SOON, FAR = [0, 1, 3, 4, 5, 7], [2, 6]


def size_of(axes):
    return int(np.prod([SIZES[NAMES.index(a)] for a in axes]))


def matmul_kernel(h_ref, *refs):
    pieces, (keep_ref, send_ref, id_ref, turned) = refs[:-4], refs[-4:]
    depth = pieces[0].shape[1]
    wide = h_ref.shape[-1]
    kept = h_ref[:, 0].reshape(-1, wide)
    sent = h_ref[:, 1].reshape(-1, wide)
    half = kept.shape[0]
    turned[:, :half] = kept[:, :depth].T
    turned[:, half:] = sent[:, :depth].T
    code = kept[:, depth:].astype(jnp.float32).T
    id_ref[...] = (code[0:1] * 256.0 + code[1:2]).astype(jnp.int32)
    for j, piece in enumerate(pieces):
        out = jnp.dot(piece[...], turned[...], preferred_element_type=jnp.float32)
        keep_ref[j] = out[:, :half]
        send_ref[j] = out[:, half:]


def partial_logits(gathered, pieces):
    nb, _, rows, _ = gathered.shape
    voc, depth = pieces[0].shape
    block = jax.ShapeDtypeStruct((len(pieces), voc, nb * rows), jnp.float32)
    vmem = pl.BlockSpec(memory_space=pltpu.VMEM)
    return pl.pallas_call(
        matmul_kernel,
        in_specs=[vmem] * (1 + len(pieces)),
        out_specs=[vmem] * 3,
        out_shape=[block, block, jax.ShapeDtypeStruct((1, nb * rows), jnp.int32)],
        scratch_shapes=[pltpu.VMEM((depth, 2 * nb * rows), gathered.dtype)],
        compiler_params=pltpu.CompilerParams(vmem_limit_bytes=51 * 1024 * 1024),
    )(gathered, *pieces)


def stats_kernel(first_ref, mine_ref, mine_far_ref, theirs_ref, theirs_far_ref, ids_ref, out_ref):
    voc, rows = mine_ref.shape[1:]
    mine = [mine_ref[SOON.index(j)] if j in SOON else mine_far_ref[FAR.index(j)] for j in range(8)]
    theirs = [
        theirs_ref[SOON.index(j ^ 1)] if j ^ 1 in SOON else theirs_far_ref[FAR.index(j ^ 1)]
        for j in range(8)
    ]
    logits = [m + t for m, t in zip(mine, theirs)]
    top = logits[0]
    for piece in logits[1:]:
        top = jnp.maximum(top, piece)
    top = jnp.max(top, axis=0, keepdims=True)
    ids = ids_ref[...]
    entry = lax.broadcasted_iota(jnp.int32, (voc, rows), 0)
    total = jnp.zeros((voc, rows), jnp.float32)
    picked = jnp.zeros((voc, rows), jnp.float32)
    for j, piece in enumerate(logits):
        total += jnp.exp(piece - top)
        picked += jnp.where(entry + first_ref[j] == ids, piece, 0.0)
    total = jnp.sum(total, axis=0, keepdims=True)
    picked = jnp.sum(picked, axis=0, keepdims=True)
    line = lax.broadcasted_iota(jnp.int32, (128, rows), 0)
    out_ref[...] = jnp.where(line == 0, top, jnp.where(line == 1, total, picked)).T


def local_stats(first, *arrays):
    vmem = pl.BlockSpec(memory_space=pltpu.VMEM)
    return pl.pallas_call(
        stats_kernel,
        in_specs=[pl.BlockSpec(memory_space=pltpu.SMEM)] + [vmem] * len(arrays),
        out_specs=vmem,
        out_shape=jax.ShapeDtypeStruct((arrays[0].shape[2], 128), jnp.float32),
        compiler_params=pltpu.CompilerParams(vmem_limit_bytes=8 * 1024 * 1024),
    )(first, *arrays)


def per_device(hidden, head_weight, target_ids, policy_logp):
    na, nb = size_of(GA), size_of(GB)
    rows, width = hidden.shape[1:]
    voc = head_weight.shape[0]
    depth = width // 2
    at = {a: lax.axis_index(a) for a in NAMES}
    k = at["x0"]

    ids = target_ids.reshape(rows, 1)
    lane = lax.broadcasted_iota(jnp.int32, (rows, IDS), 1)
    code = jnp.where(lane == 0, ids >> 8, ids & 255).astype(hidden.dtype)
    low, high = hidden[0, :, :depth], hidden[0, :, depth:]
    own = jnp.concatenate([jnp.where(k == 0, low, high), code], axis=1)
    other = jnp.concatenate([jnp.where(k == 0, high, low), code], axis=1)
    other = lax.ppermute(other, "x0", SWAP)

    kept = lax.dynamic_slice_in_dim(head_weight, k * depth, depth, 1)
    given = lax.dynamic_slice_in_dim(head_weight, (1 - k) * depth, depth, 1)
    near = lax.ppermute(given, "x0", SWAP)
    back = lax.ppermute(given, ("x1", "x0"), [(i, i ^ 3) for i in range(4)])

    message = jnp.broadcast_to(jnp.stack([own, other])[None], (na, 2, rows, depth + IDS))
    column = lax.all_to_all(message, GA, 0, 0, tiled=True)
    column = column.transpose(1, 0, 2, 3).reshape(2 * na * rows, depth + IDS)
    column, near, back = lax.optimization_barrier((column, near, back))
    copies = jnp.broadcast_to(column[None], (nb,) + column.shape)
    gathered = lax.all_to_all(copies, GB, 0, 0, tiled=True)
    gathered = gathered.reshape(nb, 2, na * rows, depth + IDS)
    far = lax.ppermute(kept, "x1", SWAP)

    soon = [kept, near, back]
    soon += [lax.ppermute(piece, "core", SWAP) for piece in soon]
    mine, send, ids = partial_logits(gathered, soon)
    theirs = lax.ppermute(send, "x0", SWAP)
    far, mine = lax.optimization_barrier((far, mine))
    late = [far, lax.ppermute(far, "core", SWAP)]
    mine_far, send_far, _ = partial_logits(gathered, late)
    theirs_far = lax.ppermute(send_far, "x0", SWAP)

    firsts = []
    for j in range(8):
        place = dict(at)
        place["x0"] = at["x0"] ^ (j & 1)
        place["x1"] = at["x1"] ^ ((j >> 1) & 1)
        place["core"] = at["core"] ^ (j >> 2)
        flat = 0
        for a, n in zip(NAMES, SIZES):
            flat = flat * n + place[a]
        firsts.append(flat * voc)
    stats = local_stats(
        jnp.stack(firsts), mine, mine_far, theirs, theirs_far, ids
    )[:, :8]
    stats = stats.reshape(nb * na, rows, 8)
    stats = lax.all_to_all(stats, GB + GA, 0, 0, tiled=True)
    tops, totals, picks = stats[..., 0], stats[..., 1], stats[..., 2]
    highest = jnp.max(tops, axis=0)
    total = jnp.sum(totals * jnp.exp(tops - highest), axis=0)
    picked = jnp.sum(picks, axis=0)
    ref_logp = (picked - (highest + jnp.log(total))).reshape(1, rows)
    log_ratio = ref_logp - policy_logp
    kl_term = jnp.minimum(jnp.exp(log_ratio) - log_ratio - 1.0, 10.0)
    return (ref_logp, kl_term)


def solution(mesh):
    fine = Mesh(mesh.devices.reshape(SIZES), NAMES)
    return jax.shard_map(
        per_device,
        mesh=fine,
        in_specs=(P(SEG, DP, None), P(SEG + DP, None), P(SEG, DP), P(SEG, DP)),
        out_specs=(P(SEG, DP), P(SEG, DP)),
        check_vma=False,
    )
```

```python
import jax
import jax.numpy as jnp
import numpy as np
from jax import lax
from jax.experimental import pallas as pl
from jax.experimental.pallas import tpu as pltpu
from jax.sharding import Mesh, PartitionSpec as P

NAMES = ("s1", "s0", "zh", "y1", "y0", "x1", "x0", "core")
SIZES = (2, 2, 2, 4, 2, 2, 2, 2)
SEG = ("s1", "s0")
DP = ("zh", "y1", "y0", "x1", "x0", "core")
GA = ("s1", "zh", "y1")
GB = ("s0", "y0")
IDS = 128
SWAP = [(0, 1), (1, 0)]
SOON, FAR = [0, 1, 3, 4, 5, 7], [2, 6]


def size_of(axes):
    return int(np.prod([SIZES[NAMES.index(a)] for a in axes]))


def matmul_kernel(h_ref, *refs):
    pieces, (keep_ref, send_ref, id_ref, turned) = refs[:-4], refs[-4:]
    depth = pieces[0].shape[1]
    wide = h_ref.shape[-1]
    kept = h_ref[:, 0].reshape(-1, wide)
    sent = h_ref[:, 1].reshape(-1, wide)
    half = kept.shape[0]
    turned[:, :half] = kept[:, :depth].T
    turned[:, half:] = sent[:, :depth].T
    code = kept[:, depth:].astype(jnp.float32).T
    id_ref[...] = (code[0:1] * 256.0 + code[1:2]).astype(jnp.int32)
    for j, piece in enumerate(pieces):
        out = jnp.dot(piece[...], turned[...], preferred_element_type=jnp.float32)
        keep_ref[j] = out[:, :half]
        send_ref[j] = out[:, half:]


def partial_logits(gathered, pieces):
    nb, _, rows, _ = gathered.shape
    voc, depth = pieces[0].shape
    block = jax.ShapeDtypeStruct((len(pieces), voc, nb * rows), jnp.float32)
    vmem = pl.BlockSpec(memory_space=pltpu.VMEM)
    return pl.pallas_call(
        matmul_kernel,
        in_specs=[vmem] * (1 + len(pieces)),
        out_specs=[vmem] * 3,
        out_shape=[block, block, jax.ShapeDtypeStruct((1, nb * rows), jnp.int32)],
        scratch_shapes=[pltpu.VMEM((depth, 2 * nb * rows), gathered.dtype)],
        compiler_params=pltpu.CompilerParams(vmem_limit_bytes=51 * 1024 * 1024),
    )(gathered, *pieces)


def stats_kernel(first_ref, mine_ref, mine_far_ref, theirs_ref, theirs_far_ref, ids_ref, out_ref):
    voc, rows = mine_ref.shape[1:]
    mine = [mine_ref[SOON.index(j)] if j in SOON else mine_far_ref[FAR.index(j)] for j in range(8)]
    theirs = [
        theirs_ref[SOON.index(j ^ 1)] if j ^ 1 in SOON else theirs_far_ref[FAR.index(j ^ 1)]
        for j in range(8)
    ]
    logits = [m + t for m, t in zip(mine, theirs)]
    top = logits[0]
    for piece in logits[1:]:
        top = jnp.maximum(top, piece)
    top = jnp.max(top, axis=0, keepdims=True)
    ids = ids_ref[...]
    entry = lax.broadcasted_iota(jnp.int32, (voc, rows), 0)
    total = jnp.zeros((voc, rows), jnp.float32)
    picked = jnp.zeros((voc, rows), jnp.float32)
    for j, piece in enumerate(logits):
        total += jnp.exp(piece - top)
        picked += jnp.where(entry + first_ref[j] == ids, piece, 0.0)
    total = jnp.sum(total, axis=0, keepdims=True)
    picked = jnp.sum(picked, axis=0, keepdims=True)
    line = lax.broadcasted_iota(jnp.int32, (128, rows), 0)
    out_ref[...] = jnp.where(line == 0, top, jnp.where(line == 1, total, picked)).T


def local_stats(first, *arrays):
    vmem = pl.BlockSpec(memory_space=pltpu.VMEM)
    return pl.pallas_call(
        stats_kernel,
        in_specs=[pl.BlockSpec(memory_space=pltpu.SMEM)] + [vmem] * len(arrays),
        out_specs=vmem,
        out_shape=jax.ShapeDtypeStruct((arrays[0].shape[2], 128), jnp.float32),
        compiler_params=pltpu.CompilerParams(vmem_limit_bytes=8 * 1024 * 1024),
    )(first, *arrays)


def finish_kernel(stats_ref, policy_ref, logp_ref, kl_ref):
    rows = stats_ref.shape[1]
    lane = lax.broadcasted_iota(jnp.int32, (1, rows), 1)
    ref_logp = jnp.zeros((1, rows), jnp.float32)
    for r in range(rows):
        tops, totals, picks = (stats_ref[:, r, c : c + 1] for c in range(3))
        highest = jnp.max(tops, axis=0, keepdims=True)
        total = jnp.sum(totals * jnp.exp(tops - highest), axis=0, keepdims=True)
        picked = jnp.sum(picks, axis=0, keepdims=True)
        ref_logp = jnp.where(lane == r, picked - (highest + jnp.log(total)), ref_logp)
    log_ratio = ref_logp - policy_ref[...]
    logp_ref[...] = ref_logp
    kl_ref[...] = jnp.minimum(jnp.exp(log_ratio) - log_ratio - 1.0, 10.0)


def finish(stats, policy_logp):
    vmem = pl.BlockSpec(memory_space=pltpu.VMEM)
    out = jax.ShapeDtypeStruct(policy_logp.shape, jnp.float32)
    return pl.pallas_call(
        finish_kernel,
        in_specs=[vmem] * 2,
        out_specs=[vmem] * 2,
        out_shape=[out, out],
        compiler_params=pltpu.CompilerParams(vmem_limit_bytes=2 * 1024 * 1024),
    )(stats, policy_logp)


def per_device(hidden, head_weight, target_ids, policy_logp):
    na, nb = size_of(GA), size_of(GB)
    rows, width = hidden.shape[1:]
    voc = head_weight.shape[0]
    depth = width // 2
    at = {a: lax.axis_index(a) for a in NAMES}
    k = at["x0"]

    ids = target_ids.reshape(rows, 1)
    lane = lax.broadcasted_iota(jnp.int32, (rows, IDS), 1)
    code = jnp.where(lane == 0, ids >> 8, ids & 255).astype(hidden.dtype)
    low, high = hidden[0, :, :depth], hidden[0, :, depth:]
    own = jnp.concatenate([jnp.where(k == 0, low, high), code], axis=1)
    other = jnp.concatenate([jnp.where(k == 0, high, low), code], axis=1)
    other = lax.ppermute(other, "x0", SWAP)

    kept = lax.dynamic_slice_in_dim(head_weight, k * depth, depth, 1)
    given = lax.dynamic_slice_in_dim(head_weight, (1 - k) * depth, depth, 1)
    near = lax.ppermute(given, "x0", SWAP)
    back = lax.ppermute(given, ("x1", "x0"), [(i, i ^ 3) for i in range(4)])

    message = jnp.broadcast_to(jnp.stack([own, other])[None], (na, 2, rows, depth + IDS))
    column = lax.all_to_all(message, GA, 0, 0, tiled=True)
    column = column.transpose(1, 0, 2, 3).reshape(2 * na * rows, depth + IDS)
    column, near, back = lax.optimization_barrier((column, near, back))
    copies = jnp.broadcast_to(column[None], (nb,) + column.shape)
    gathered = lax.all_to_all(copies, GB, 0, 0, tiled=True)
    gathered = gathered.reshape(nb, 2, na * rows, depth + IDS)
    far = lax.ppermute(kept, "x1", SWAP)

    gathered, far = lax.optimization_barrier((gathered, far))
    soon = [kept, near, back]
    soon += [lax.ppermute(piece, "core", SWAP) for piece in soon]
    mine, send, ids = partial_logits(gathered, soon)
    theirs = lax.ppermute(send, "x0", SWAP)
    far, mine = lax.optimization_barrier((far, mine))
    late = [far, lax.ppermute(far, "core", SWAP)]
    mine_far, send_far, _ = partial_logits(gathered, late)
    theirs_far = lax.ppermute(send_far, "x0", SWAP)

    firsts = []
    for j in range(8):
        place = dict(at)
        place["x0"] = at["x0"] ^ (j & 1)
        place["x1"] = at["x1"] ^ ((j >> 1) & 1)
        place["core"] = at["core"] ^ (j >> 2)
        flat = 0
        for a, n in zip(NAMES, SIZES):
            flat = flat * n + place[a]
        firsts.append(flat * voc)
    stats = local_stats(
        jnp.stack(firsts), mine, mine_far, theirs, theirs_far, ids
    )[:, :8]
    stats = stats.reshape(nb * na, rows, 8)
    stats = lax.all_to_all(stats, GB + GA, 0, 0, tiled=True)
    return tuple(finish(stats, policy_logp))


def solution(mesh):
    fine = Mesh(mesh.devices.reshape(SIZES), NAMES)
    return jax.shard_map(
        per_device,
        mesh=fine,
        in_specs=(P(SEG, DP, None), P(SEG + DP, None), P(SEG, DP), P(SEG, DP)),
        out_specs=(P(SEG, DP), P(SEG, DP)),
        check_vma=False,
    )
```

```python
import jax
import jax.numpy as jnp
import numpy as np
from jax import lax
from jax.experimental import pallas as pl
from jax.experimental.pallas import tpu as pltpu
from jax.sharding import Mesh, PartitionSpec as P

NAMES = ("s1", "s0", "zh", "y1", "y0", "x1", "x0", "core")
SIZES = (2, 2, 2, 4, 2, 2, 2, 2)
SEG = ("s1", "s0")
DP = ("zh", "y1", "y0", "x1", "x0", "core")
GA = ("s1", "zh", "y1")
GB = ("s0", "y0")
IDS = 128
SWAP = [(0, 1), (1, 0)]
SOON, FAR = [0, 1, 3, 4, 5, 7], [2, 6]


def size_of(axes):
    return int(np.prod([SIZES[NAMES.index(a)] for a in axes]))


def matmul_kernel(h_ref, *refs):
    pieces, (keep_ref, send_ref, id_ref, turned) = refs[:-4], refs[-4:]
    depth = pieces[0].shape[1]
    wide = h_ref.shape[-1]
    kept = h_ref[:, 0].reshape(-1, wide)
    sent = h_ref[:, 1].reshape(-1, wide)
    half = kept.shape[0]
    turned[:, :half] = kept[:, :depth].T
    turned[:, half:] = sent[:, :depth].T
    code = kept[:, depth:].astype(jnp.float32).T
    id_ref[...] = (code[0:1] * 256.0 + code[1:2]).astype(jnp.int32)
    for j, piece in enumerate(pieces):
        out = jnp.dot(piece[...], turned[...], preferred_element_type=jnp.float32)
        keep_ref[j] = out[:, :half]
        send_ref[j] = out[:, half:]


def partial_logits(gathered, pieces):
    nb, _, rows, _ = gathered.shape
    voc, depth = pieces[0].shape
    block = jax.ShapeDtypeStruct((len(pieces), voc, nb * rows), jnp.float32)
    vmem = pl.BlockSpec(memory_space=pltpu.VMEM)
    return pl.pallas_call(
        matmul_kernel,
        in_specs=[vmem] * (1 + len(pieces)),
        out_specs=[vmem] * 3,
        out_shape=[block, block, jax.ShapeDtypeStruct((1, nb * rows), jnp.int32)],
        scratch_shapes=[pltpu.VMEM((depth, 2 * nb * rows), gathered.dtype)],
        compiler_params=pltpu.CompilerParams(vmem_limit_bytes=51 * 1024 * 1024),
    )(gathered, *pieces)


def stats_kernel(first_ref, mine_ref, mine_far_ref, theirs_ref, theirs_far_ref, ids_ref, out_ref):
    voc, rows = mine_ref.shape[1:]
    mine = [mine_ref[SOON.index(j)] if j in SOON else mine_far_ref[FAR.index(j)] for j in range(8)]
    theirs = [
        theirs_ref[SOON.index(j ^ 1)] if j ^ 1 in SOON else theirs_far_ref[FAR.index(j ^ 1)]
        for j in range(8)
    ]
    logits = [m + t for m, t in zip(mine, theirs)]
    top = logits[0]
    for piece in logits[1:]:
        top = jnp.maximum(top, piece)
    top = jnp.max(top, axis=0, keepdims=True)
    ids = ids_ref[...]
    entry = lax.broadcasted_iota(jnp.int32, (voc, rows), 0)
    total = jnp.zeros((voc, rows), jnp.float32)
    picked = jnp.zeros((voc, rows), jnp.float32)
    for j, piece in enumerate(logits):
        total += jnp.exp(piece - top)
        picked += jnp.where(entry + first_ref[j] == ids, piece, 0.0)
    total = jnp.sum(total, axis=0, keepdims=True)
    picked = jnp.sum(picked, axis=0, keepdims=True)
    line = lax.broadcasted_iota(jnp.int32, (128, rows), 0)
    out_ref[...] = jnp.where(line == 0, top, jnp.where(line == 1, total, picked)).T


def local_stats(first, *arrays):
    vmem = pl.BlockSpec(memory_space=pltpu.VMEM)
    return pl.pallas_call(
        stats_kernel,
        in_specs=[pl.BlockSpec(memory_space=pltpu.SMEM)] + [vmem] * len(arrays),
        out_specs=vmem,
        out_shape=jax.ShapeDtypeStruct((arrays[0].shape[2], 128), jnp.float32),
        compiler_params=pltpu.CompilerParams(vmem_limit_bytes=8 * 1024 * 1024),
    )(first, *arrays)


def finish_kernel(stats_ref, policy_ref, logp_ref, kl_ref):
    rows = stats_ref.shape[1]
    lane = lax.broadcasted_iota(jnp.int32, (1, rows), 1)
    ref_logp = jnp.zeros((1, rows), jnp.float32)
    for r in range(rows):
        tops, totals, picks = (stats_ref[:, r, c : c + 1] for c in range(3))
        highest = jnp.max(tops, axis=0, keepdims=True)
        total = jnp.sum(totals * jnp.exp(tops - highest), axis=0, keepdims=True)
        picked = jnp.sum(picks, axis=0, keepdims=True)
        ref_logp = jnp.where(lane == r, picked - (highest + jnp.log(total)), ref_logp)
    log_ratio = ref_logp - policy_ref[...]
    logp_ref[...] = ref_logp
    kl_ref[...] = jnp.minimum(jnp.exp(log_ratio) - log_ratio - 1.0, 10.0)


def finish(stats, policy_logp):
    vmem = pl.BlockSpec(memory_space=pltpu.VMEM)
    out = jax.ShapeDtypeStruct(policy_logp.shape, jnp.float32)
    return pl.pallas_call(
        finish_kernel,
        in_specs=[vmem] * 2,
        out_specs=[vmem] * 2,
        out_shape=[out, out],
        compiler_params=pltpu.CompilerParams(vmem_limit_bytes=2 * 1024 * 1024),
    )(stats, policy_logp)


def per_device(hidden, head_weight, target_ids, policy_logp):
    na, nb = size_of(GA), size_of(GB)
    rows, width = hidden.shape[1:]
    voc = head_weight.shape[0]
    depth = width // 2
    at = {a: lax.axis_index(a) for a in NAMES}
    k = at["x0"]

    lane = lax.broadcasted_iota(jnp.int32, (rows, IDS), 1)
    ids = jnp.broadcast_to(target_ids.reshape(rows, 1), (rows, IDS))
    code = jnp.where(lane == 0, ids >> 8, ids & 255).astype(hidden.dtype)
    own = lax.dynamic_slice_in_dim(hidden[0], k * depth, depth, 1)
    other = lax.dynamic_slice_in_dim(hidden[0], (1 - k) * depth, depth, 1)
    own = jnp.concatenate([own, code], axis=1)
    other = jnp.concatenate([other, code], axis=1)
    other = lax.ppermute(other, "x0", SWAP)

    kept = lax.dynamic_slice_in_dim(head_weight, k * depth, depth, 1)
    given = lax.dynamic_slice_in_dim(head_weight, (1 - k) * depth, depth, 1)
    near = lax.ppermute(given, "x0", SWAP)
    back = lax.ppermute(given, ("x1", "x0"), [(i, i ^ 3) for i in range(4)])

    message = jnp.broadcast_to(jnp.stack([own, other])[None], (na, 2, rows, depth + IDS))
    column = lax.all_to_all(message, GA, 0, 0, tiled=True)
    column = column.transpose(1, 0, 2, 3).reshape(2 * na * rows, depth + IDS)
    column, near, back = lax.optimization_barrier((column, near, back))
    copies = jnp.broadcast_to(column[None], (nb,) + column.shape)
    gathered = lax.all_to_all(copies, GB, 0, 0, tiled=True)
    gathered = gathered.reshape(nb, 2, na * rows, depth + IDS)
    far = lax.ppermute(kept, "x1", SWAP)

    gathered, far = lax.optimization_barrier((gathered, far))
    soon = [kept, near, back]
    soon += [lax.ppermute(piece, "core", SWAP) for piece in soon]
    mine, send, ids = partial_logits(gathered, soon)
    theirs = lax.ppermute(send, "x0", SWAP)
    late = [far, lax.ppermute(far, "core", SWAP)]
    mine_far, send_far, _ = partial_logits(gathered, late)
    theirs_far = lax.ppermute(send_far, "x0", SWAP)

    firsts = []
    for j in range(8):
        place = dict(at)
        place["x0"] = at["x0"] ^ (j & 1)
        place["x1"] = at["x1"] ^ ((j >> 1) & 1)
        place["core"] = at["core"] ^ (j >> 2)
        flat = 0
        for a, n in zip(NAMES, SIZES):
            flat = flat * n + place[a]
        firsts.append(flat * voc)
    stats = local_stats(
        jnp.stack(firsts), mine, mine_far, theirs, theirs_far, ids
    )[:, :8]
    stats = stats.reshape(nb * na, rows, 8)
    stats = lax.all_to_all(stats, GB + GA, 0, 0, tiled=True)
    return tuple(finish(stats, policy_logp))


def solution(mesh):
    fine = Mesh(mesh.devices.reshape(SIZES), NAMES)
    return jax.shard_map(
        per_device,
        mesh=fine,
        in_specs=(P(SEG, DP, None), P(SEG + DP, None), P(SEG, DP), P(SEG, DP)),
        out_specs=(P(SEG, DP), P(SEG, DP)),
        check_vma=False,
    )
```

```python
import jax
import jax.numpy as jnp
import numpy as np
from jax import lax
from jax.experimental import pallas as pl
from jax.experimental.pallas import tpu as pltpu
from jax.sharding import Mesh, PartitionSpec as P

NAMES = ("s1", "s0", "zh", "y1", "y0", "x1", "x0", "core")
SIZES = (2, 2, 2, 4, 2, 2, 2, 2)
SEG = ("s1", "s0")
DP = ("zh", "y1", "y0", "x1", "x0", "core")
GA = ("s1", "zh", "y1")
GB = ("s0", "y0")
IDS = 128
SWAP = [(0, 1), (1, 0)]
SOON, FAR = [0, 1, 3, 4, 5, 7], [2, 6]


def size_of(axes):
    return int(np.prod([SIZES[NAMES.index(a)] for a in axes]))


def matmul_kernel(h_ref, *refs):
    pieces, (keep_ref, send_ref, id_ref, turned) = refs[:-4], refs[-4:]
    depth = pieces[0].shape[1]
    wide = h_ref.shape[-1]
    kept = h_ref[:, 0].reshape(-1, wide)
    sent = h_ref[:, 1].reshape(-1, wide)
    half = kept.shape[0]
    turned[:, :half] = kept[:, :depth].T
    turned[:, half:] = sent[:, :depth].T
    code = kept[:, depth:].astype(jnp.float32).T
    id_ref[...] = (code[0:1] * 256.0 + code[1:2]).astype(jnp.int32)
    for j, piece in enumerate(pieces):
        out = jnp.dot(piece[...], turned[...], preferred_element_type=jnp.float32)
        keep_ref[j] = out[:, :half]
        send_ref[j] = out[:, half:]


def partial_logits(gathered, pieces):
    nb, _, rows, _ = gathered.shape
    voc, depth = pieces[0].shape
    block = jax.ShapeDtypeStruct((len(pieces), voc, nb * rows), jnp.float32)
    vmem = pl.BlockSpec(memory_space=pltpu.VMEM)
    return pl.pallas_call(
        matmul_kernel,
        in_specs=[vmem] * (1 + len(pieces)),
        out_specs=[vmem] * 3,
        out_shape=[block, block, jax.ShapeDtypeStruct((1, nb * rows), jnp.int32)],
        scratch_shapes=[pltpu.VMEM((depth, 2 * nb * rows), gathered.dtype)],
        compiler_params=pltpu.CompilerParams(vmem_limit_bytes=51 * 1024 * 1024),
    )(gathered, *pieces)


def far_kernel(h_ref, first_ref, second_ref, keep_ref, send_ref):
    voc, depth = first_ref.shape
    wide = h_ref.shape[-1]
    rows = [h_ref[:, i].reshape(-1, wide)[:, :depth] for i in range(2)]
    half = rows[0].shape[0]
    weights = jnp.concatenate([first_ref[...], second_ref[...]], axis=0)
    out = lax.dot_general(
        jnp.concatenate(rows, axis=0),
        weights,
        (((1,), (1,)), ((), ())),
        preferred_element_type=jnp.float32,
    ).T
    for j in range(2):
        keep_ref[j] = out[j * voc : (j + 1) * voc, :half]
        send_ref[j] = out[j * voc : (j + 1) * voc, half:]


def far_logits(gathered, pieces):
    nb, _, rows, _ = gathered.shape
    block = jax.ShapeDtypeStruct((2, pieces[0].shape[0], nb * rows), jnp.float32)
    vmem = pl.BlockSpec(memory_space=pltpu.VMEM)
    return pl.pallas_call(
        far_kernel,
        in_specs=[vmem] * 3,
        out_specs=[vmem] * 2,
        out_shape=[block, block],
        compiler_params=pltpu.CompilerParams(vmem_limit_bytes=51 * 1024 * 1024),
    )(gathered, *pieces)


def stats_kernel(first_ref, mine_ref, mine_far_ref, theirs_ref, theirs_far_ref, ids_ref, out_ref):
    voc, rows = mine_ref.shape[1:]
    mine = [mine_ref[SOON.index(j)] if j in SOON else mine_far_ref[FAR.index(j)] for j in range(8)]
    theirs = [
        theirs_ref[SOON.index(j ^ 1)] if j ^ 1 in SOON else theirs_far_ref[FAR.index(j ^ 1)]
        for j in range(8)
    ]
    logits = [m + t for m, t in zip(mine, theirs)]
    top = logits[0]
    for piece in logits[1:]:
        top = jnp.maximum(top, piece)
    top = jnp.max(top, axis=0, keepdims=True)
    ids = ids_ref[...]
    entry = lax.broadcasted_iota(jnp.int32, (voc, rows), 0)
    total = jnp.zeros((voc, rows), jnp.float32)
    picked = jnp.zeros((voc, rows), jnp.float32)
    for j, piece in enumerate(logits):
        total += jnp.exp(piece - top)
        picked += jnp.where(entry + first_ref[j] == ids, piece, 0.0)
    total = jnp.sum(total, axis=0, keepdims=True)
    picked = jnp.sum(picked, axis=0, keepdims=True)
    line = lax.broadcasted_iota(jnp.int32, (128, rows), 0)
    out_ref[...] = jnp.where(line == 0, top, jnp.where(line == 1, total, picked)).T


def local_stats(first, *arrays):
    vmem = pl.BlockSpec(memory_space=pltpu.VMEM)
    return pl.pallas_call(
        stats_kernel,
        in_specs=[pl.BlockSpec(memory_space=pltpu.SMEM)] + [vmem] * len(arrays),
        out_specs=vmem,
        out_shape=jax.ShapeDtypeStruct((arrays[0].shape[2], 128), jnp.float32),
        compiler_params=pltpu.CompilerParams(vmem_limit_bytes=8 * 1024 * 1024),
    )(first, *arrays)


def finish_kernel(stats_ref, policy_ref, logp_ref, kl_ref):
    rows = stats_ref.shape[1]
    lane = lax.broadcasted_iota(jnp.int32, (1, rows), 1)
    ref_logp = jnp.zeros((1, rows), jnp.float32)
    for r in range(rows):
        tops, totals, picks = (stats_ref[:, r, c : c + 1] for c in range(3))
        highest = jnp.max(tops, axis=0, keepdims=True)
        total = jnp.sum(totals * jnp.exp(tops - highest), axis=0, keepdims=True)
        picked = jnp.sum(picks, axis=0, keepdims=True)
        ref_logp = jnp.where(lane == r, picked - (highest + jnp.log(total)), ref_logp)
    log_ratio = ref_logp - policy_ref[...]
    logp_ref[...] = ref_logp
    kl_ref[...] = jnp.minimum(jnp.exp(log_ratio) - log_ratio - 1.0, 10.0)


def finish(stats, policy_logp):
    vmem = pl.BlockSpec(memory_space=pltpu.VMEM)
    out = jax.ShapeDtypeStruct(policy_logp.shape, jnp.float32)
    return pl.pallas_call(
        finish_kernel,
        in_specs=[vmem] * 2,
        out_specs=[vmem] * 2,
        out_shape=[out, out],
        compiler_params=pltpu.CompilerParams(vmem_limit_bytes=2 * 1024 * 1024),
    )(stats, policy_logp)


def per_device(hidden, head_weight, target_ids, policy_logp):
    na, nb = size_of(GA), size_of(GB)
    rows, width = hidden.shape[1:]
    voc = head_weight.shape[0]
    depth = width // 2
    at = {a: lax.axis_index(a) for a in NAMES}
    k = at["x0"]

    ids = target_ids.reshape(rows, 1)
    lane = lax.broadcasted_iota(jnp.int32, (rows, IDS), 1)
    code = jnp.where(lane == 0, ids >> 8, ids & 255).astype(hidden.dtype)
    low, high = hidden[0, :, :depth], hidden[0, :, depth:]
    own = jnp.concatenate([jnp.where(k == 0, low, high), code], axis=1)
    other = jnp.concatenate([jnp.where(k == 0, high, low), code], axis=1)
    other = lax.ppermute(other, "x0", SWAP)

    kept = lax.dynamic_slice_in_dim(head_weight, k * depth, depth, 1)
    given = lax.dynamic_slice_in_dim(head_weight, (1 - k) * depth, depth, 1)
    near = lax.ppermute(given, "x0", SWAP)
    back = lax.ppermute(given, ("x1", "x0"), [(i, i ^ 3) for i in range(4)])

    message = jnp.broadcast_to(jnp.stack([own, other])[None], (na, 2, rows, depth + IDS))
    column = lax.all_to_all(message, GA, 0, 0, tiled=True)
    column = column.transpose(1, 0, 2, 3).reshape(2 * na * rows, depth + IDS)
    column, near, back = lax.optimization_barrier((column, near, back))
    copies = jnp.broadcast_to(column[None], (nb,) + column.shape)
    gathered = lax.all_to_all(copies, GB, 0, 0, tiled=True)
    gathered = gathered.reshape(nb, 2, na * rows, depth + IDS)
    far = lax.ppermute(kept, "x1", SWAP)

    gathered, far = lax.optimization_barrier((gathered, far))
    soon = [kept, near, back]
    soon += [lax.ppermute(piece, "core", SWAP) for piece in soon]
    mine, send, ids = partial_logits(gathered, soon)
    theirs = lax.ppermute(send, "x0", SWAP)
    far, mine = lax.optimization_barrier((far, mine))
    late = [far, lax.ppermute(far, "core", SWAP)]
    mine_far, send_far = far_logits(gathered, late)
    theirs_far = lax.ppermute(send_far, "x0", SWAP)

    firsts = []
    for j in range(8):
        place = dict(at)
        place["x0"] = at["x0"] ^ (j & 1)
        place["x1"] = at["x1"] ^ ((j >> 1) & 1)
        place["core"] = at["core"] ^ (j >> 2)
        flat = 0
        for a, n in zip(NAMES, SIZES):
            flat = flat * n + place[a]
        firsts.append(flat * voc)
    stats = local_stats(
        jnp.stack(firsts), mine, mine_far, theirs, theirs_far, ids
    )[:, :8]
    stats = stats.reshape(nb * na, rows, 8)
    stats = lax.all_to_all(stats, GB + GA, 0, 0, tiled=True)
    return tuple(finish(stats, policy_logp))


def solution(mesh):
    fine = Mesh(mesh.devices.reshape(SIZES), NAMES)
    return jax.shard_map(
        per_device,
        mesh=fine,
        in_specs=(P(SEG, DP, None), P(SEG + DP, None), P(SEG, DP), P(SEG, DP)),
        out_specs=(P(SEG, DP), P(SEG, DP)),
        check_vma=False,
    )
```
